128 devices in a mesh: src: 8 (over y, x_lo), tgt: 16 (over z, x_hi, core).
Axes of the slice: x: 4 (x_hi: 2, x_lo: 2; x = x_hi * 2 + x_lo), y: 4, z: 4, core: 2. Of those that a mesh axis runs over, the one named last changes fastest.
Arguments:
- coeffs: bfloat16 [8, 16, 16, 128, 256], P('src', 'tgt'), may hold values from -6 to 6
- weights: bfloat16 [8, 16, 16, 11, 64, 256], P('src', 'tgt'), may hold values from -0.375 to 0.375
- evaluate: bfloat16 [16, 16, 8, 1024, 128], P('tgt', 'src'), may hold values from -0.1875 to 0.1875
Outputs:
- field_image: bfloat16 [16, 16, 1024, 256], P('tgt', 'src')
The draws below stay inside these ranges and needn't reach their ends.
All inputs are finite; a program needn't handle non-finite values.
Results may differ from the reference program's by a relative error of at most 0.024.
Values may be sent and summed in bfloat16 or wider, within the bound.
No kernel may reach another device: no remote copies, remote signals or barrier semaphores. Data moves between devices by JAX's collectives and lax.ppermute only.
A program may use at most 64 MiB of HBM per device.

```python
import jax
import jax.numpy as jnp
from jax import lax

R = 64
S = 256
LOC = 16
PTS = 1024
LBITS = 4
SBITS = 3
TBITS = 4
LEVELS = 11
N_SRC = 8
N_TGT = 16


def level_of(own_key, dims, cuts, low, largest):
    def one(axis_at, blocks):
        draws = jax.random.uniform(jax.random.fold_in(jax.random.fold_in(own_key, 6), axis_at), (blocks,), jnp.float32, low / len(cuts), largest / len(cuts))
        return jnp.repeat(jnp.exp(draws), dims[axis_at] // blocks).reshape((-1,) + (1,) * (len(dims) - axis_at - 1))

    loudness = one(*cuts[0])
    for cut in cuts[1:]:
        loudness = loudness * one(*cut)
    return loudness


def scatter_about(own_key, dims, width, most, split=(), dtype=jnp.bfloat16):
    values = jax.random.normal(own_key, dims, jnp.float32) * width
    if len(split) > 0:
        values = level_of(own_key, dims, split, -0.22, 0.18) * values
    return jnp.clip(values, min=-most, max=most).astype(dtype)


def setup_inputs(seed: int = 0) -> dict:
    key_of = jax.random.split(jax.random.key(seed), 4)
    return {
        "coeffs": scatter_about(key_of[0], (N_SRC, N_TGT, LOC, 2 * R, S), 1.0, 6.0, ((0, 8), (1, 16))),
        "weights": scatter_about(key_of[1], (N_SRC, N_TGT, LOC, LEVELS, R, 4 * R), (4 * R) ** -0.5, 0.375, ((0, 8), (1, 16))),
        "evaluate": scatter_about(key_of[2], (N_TGT, LOC, N_SRC, PTS, 2 * R), (2 * R * N_SRC) ** -0.5, 0.1875, ((0, 16), (1, 8))),
    }


def flip_bit(values, axis_pos, bit_index):
    full_shape = values.shape
    dim_count = full_shape[axis_pos]
    split_view = values.reshape(full_shape[:axis_pos] + (dim_count >> (bit_index + 1), 2, 1 << bit_index) + full_shape[axis_pos + 1:])
    return jnp.flip(split_view, axis_pos + 1).reshape(full_shape)


def complex_products(weight_pair, coefficients):
    box_count, rank_size = weight_pair.shape[0], weight_pair.shape[1]
    real_imag = coefficients.reshape(box_count, 2, rank_size, -1).astype(jnp.float32)
    products_all = jnp.einsum("brkj,bmjs->bkmrs", weight_pair.astype(jnp.float32), real_imag)
    return products_all[:, 0, 0] - products_all[:, 1, 1], products_all[:, 0, 1] + products_all[:, 1, 0]


def apply_level(level_weights, coefficients, partner):
    box_count, rank_size = level_weights.shape[0], level_weights.shape[1]
    blocks = level_weights.reshape(box_count, rank_size, 4, rank_size)
    own_real, own_imag = complex_products(blocks[:, :, 0:2], coefficients)
    far_real, far_imag = complex_products(blocks[:, :, 2:4], partner)
    return jnp.concatenate([own_real + far_real, own_imag + far_imag], axis=1).astype(jnp.bfloat16)


def reference(coeffs, weights, evaluate):
    level_order = [(2, bit_index) for bit_index in range(LBITS)]
    for bit_index in range(max(SBITS, TBITS)):
        if bit_index < TBITS:
            level_order.append((1, bit_index))
        if bit_index < SBITS:
            level_order.append((0, bit_index))
    values = coeffs
    for level_index, (axis_pos, bit_index) in enumerate(level_order):
        partner = flip_bit(values, axis_pos, bit_index)
        level_weights = weights[:, :, :, level_index]

        def per_source(pieces):
            weight_block, coef_block, partner_block = pieces
            inner_shape = coef_block.shape
            result = apply_level(weight_block.reshape((-1,) + weight_block.shape[2:]),
                                 coef_block.reshape((-1,) + inner_shape[2:]),
                                 partner_block.reshape((-1,) + inner_shape[2:]))
            return result.reshape(inner_shape)

        values = lax.map(per_source, (level_weights, values, partner))
    by_target = jnp.transpose(values, (1, 2, 0, 3, 4))

    def per_target(pieces):
        eval_block, coef_block = pieces
        summed = jnp.einsum("bspj,bsjq->bpq", eval_block.astype(jnp.float32), coef_block.astype(jnp.float32))
        return summed.astype(jnp.bfloat16)

    return lax.map(per_target, (evaluate, by_target))
```

```python
import jax
import jax.numpy as jnp
from jax import lax
from jax.experimental import pallas as pl
from jax.experimental.pallas import tpu as pltpu
from jax.sharding import PartitionSpec as P

BF16 = jnp.bfloat16
LIMIT = 40 * 1024 * 1024
LOCAL = 4
FIRST = (0, 1)
STEPS = (
    (6, (0, 1)),
    (6, (0, 0)),
    (7, (0, 1)),
    (6, (1, 1)),
    (7, (0, 0)),
    (6, (1, 0)),
    (7, (1, 1)),
    (8, (0, 1)),
    (7, (1, 0)),
    (8, (0, 0)),
    (9, (0, 1)),
    (8, (1, 1)),
    (9, (0, 0)),
    (8, (1, 0)),
    (9, (1, 1)),
    (10, (0, 1)),
    (9, (1, 0)),
    (10, (0, 0)),
    (11, 0),
    (10, (1, 1)),
    (10, (1, 0)),
    (11, 1),
)


def stacked(w):
    n = w.shape[0]
    parts = [w[:, i * n : (i + 1) * n] for i in range(4)]
    top = jnp.concatenate([parts[0], -parts[1], parts[2], -parts[3]], axis=1)
    low = jnp.concatenate([parts[1], parts[0], parts[3], parts[2]], axis=1)
    return jnp.concatenate([top, low], axis=0)


def combine(w, own, partner):
    both = jnp.concatenate([own, partner], axis=0)
    return jnp.dot(stacked(w), both, preferred_element_type=jnp.float32).astype(BF16)


def combine_pair(wa, wb, xa, xb):
    n = 2 * wa.shape[0]
    first, second = stacked(wa), stacked(wb)
    second = jnp.concatenate([second[:, n:], second[:, :n]], axis=1)
    lhs = jnp.concatenate([first, second], axis=0)
    out = jnp.dot(lhs, jnp.concatenate([xa, xb], axis=0), preferred_element_type=jnp.float32)
    out = out.astype(BF16)
    return out[:n], out[n:]


def call(body, out_shapes, args, specs=None, scratch=(), flops=0, moved=0):
    return pl.pallas_call(
        body,
        out_shape=[jax.ShapeDtypeStruct(s, BF16) for s in out_shapes],
        in_specs=specs or [pl.BlockSpec(memory_space=pltpu.VMEM)] * len(args),
        out_specs=[pl.BlockSpec(memory_space=pltpu.VMEM)] * len(out_shapes),
        scratch_shapes=list(scratch),
        cost_estimate=pl.CostEstimate(flops=flops, bytes_accessed=moved, transcendentals=0),
        compiler_params=pltpu.CompilerParams(vmem_limit_bytes=LIMIT),
    )(*args)


class Order:
    def __init__(self):
        self.last = None

    def level(self, arrays, weights, outs, paired=False, after=()):
        na, nw = len(arrays), len(weights)
        rows, shots = arrays[0].shape[1:]

        def body(*refs):
            x, w, o = refs[:na], refs[na : na + nw], refs[len(args) :]
            get = lambda refs, at: refs[at[0]][at[1]]
            for k, jobs in enumerate(outs):
                if paired:
                    for i in range(0, len(jobs), 2):
                        (xa, xb, wa), (_, _, wb) = jobs[i], jobs[i + 1]
                        o[k][i], o[k][i + 1] = combine_pair(get(w, wa), get(w, wb), get(x, xa), get(x, xb))
                else:
                    for i, (xa, xb, wa) in enumerate(jobs):
                        o[k][i] = combine(get(w, wa), get(x, xa), get(x, xb))

        args = list(arrays) + list(weights) + list(after)
        if self.last is not None:
            args.append(self.last)
        jobs = sum(len(j) for j in outs)
        results = call(
            body,
            [(len(j), rows, shots) for j in outs],
            args,
            flops=2 * jobs * rows * 2 * rows * shots,
            moved=jobs * rows * shots * 4,
        )
        self.last = results[0]
        return results

    def split_weights(self, weights):
        rank, cols = weights.shape[2:]
        pair = (2, rank, cols)

        def body(w, _, keep78, keep9, send1, send2, send3, sems):
            flip = lax.axis_index("src") * 2
            copies = []

            def put(src_box, first, dst):
                sem = sems.at[len(copies)]
                copies.append(pltpu.make_async_copy(w.at[src_box, pl.ds(first, 2)], dst, sem))

            for b2 in (1, 0):
                for b3 in range(2):
                    for q in range(4):
                        b1, b0 = q >> 1, q & 1
                        box = jnp.bitwise_xor(b0 + 2 * b1 + 4 * b2 + 8 * b3, flip)
                        put(box, 7, (send1 if b2 else keep78).at[b3 * 4 + q])
                        if b3:
                            put(box, 9, (send3 if b2 else send2).at[q])
                        else:
                            put(box, 9, send1.at[8 + q] if b2 else keep9.at[q])
            for c in copies:
                c.start()
            for c in copies:
                c.wait()

        results = call(
            body,
            [(8,) + pair, (4,) + pair, (12,) + pair, (4,) + pair, (4,) + pair],
            [weights, self.last],
            specs=[pl.BlockSpec(memory_space=pltpu.HBM), pl.BlockSpec(memory_space=pltpu.VMEM)],
            scratch=[pltpu.SemaphoreType.DMA((32,))],
            moved=16 * 4 * rank * cols * 4,
        )
        self.last = results[0]
        return results

    def local_levels(self, coeffs, weights):
        loc, rows, shots = coeffs.shape
        rank, cols = weights.shape[2:]

        def body(x_hbm, w, out0, out1, early, x, wbuf, buf, sem, sems, early_sems):
            flip = lax.axis_index("src") * 2

            def actual(r):
                b0, b1, b2, b3 = r >> 3, (r >> 2) & 1, (r >> 1) & 1, r & 1
                return jnp.bitwise_xor(b0 + 2 * b1 + 4 * b2 + 8 * b3, flip)

            fetch = pltpu.make_async_copy(x_hbm, x, sem)
            fetch.start()
            copies = [
                pltpu.make_async_copy(w.at[:, l], wbuf.at[l], sems.at[l]) for l in range(LOCAL)
            ]
            for c in copies:
                c.start()
            later = [
                pltpu.make_async_copy(w.at[actual(r), pl.ds(LOCAL, 3)], early.at[r], early_sems.at[r])
                for r in range(loc)
            ]
            for c in later:
                c.start()
            fetch.wait()
            for l in range(LOCAL):
                copies[l].wait()
                src = x if l == 0 else buf.at[(l - 1) % 2]
                dst = buf.at[l % 2]
                if l < LOCAL - 1:
                    for b in range(loc):
                        far = b ^ (1 << l)
                        if b < far:
                            dst[b], dst[far] = combine_pair(wbuf[l, b], wbuf[l, far], src[b], src[far])
                else:
                    for r in range(0, loc, 2):
                        b, far = actual(r), actual(r + 1)
                        out = out1 if r >= loc // 2 else out0
                        i = r % (loc // 2)
                        out[i], out[i + 1] = combine_pair(wbuf[l, b], wbuf[l, far], src[b], src[far])
            for c in later:
                c.wait()

        results = call(
            body,
            [(loc // 2, rows, shots)] * 2 + [(loc, 3, rank, cols)],
            [coeffs, weights],
            specs=[pl.BlockSpec(memory_space=pltpu.HBM)] * 2,
            scratch=[
                pltpu.VMEM((loc, rows, shots), BF16),
                pltpu.VMEM((LOCAL, loc, rank, cols), BF16),
                pltpu.VMEM((2, loc, rows, shots), BF16),
                pltpu.SemaphoreType.DMA,
                pltpu.SemaphoreType.DMA((LOCAL,)),
                pltpu.SemaphoreType.DMA((loc,)),
            ],
            flops=2 * LOCAL * loc * rows * 2 * rows * shots,
            moved=LOCAL * loc * rank * cols * 2,
        )
        self.last = results[0]
        return results

    def evaluated(self, evaluate, kept, came, box, field):
        boxes, sources, points, rows = evaluate.shape
        shots = kept.shape[2]
        tile = 256

        def body(e, k, c, _, out, buf, sems):
            me = lax.axis_index("src")
            copies = []
            for i in range(points // tile):
                rng = slice(i * tile, (i + 1) * tile)
                total = jnp.zeros((tile, shots), jnp.float32)
                for pair in range(sources // 2):
                    b2, b1 = pair >> 1, pair & 1
                    near = jnp.bitwise_xor(me, 2 * b1 + 4 * b2)
                    far = jnp.bitwise_xor(near, 1)
                    lhs = jnp.concatenate([e[box, near, rng], e[box, far, rng]], axis=1)
                    rhs = jnp.concatenate([k[pair], c[pair]], axis=0)
                    total += jnp.dot(lhs, rhs, preferred_element_type=jnp.float32)
                buf[i] = total.astype(BF16)
                copies.append(pltpu.make_async_copy(buf.at[i], out.at[box, pl.ds(i * tile, tile)], sems.at[i]))
                copies[-1].start()
            for copy in copies:
                copy.wait()

        vmem = pl.BlockSpec(memory_space=pltpu.VMEM)
        hbm = pl.BlockSpec(memory_space=pltpu.HBM)
        out = pl.pallas_call(
            body,
            out_shape=jax.ShapeDtypeStruct((boxes, points, shots), BF16),
            in_specs=[vmem, vmem, vmem, vmem if field is None else hbm],
            out_specs=hbm,
            input_output_aliases={} if field is None else {3: 0},
            scratch_shapes=[
                pltpu.VMEM((points // tile, tile, shots), BF16),
                pltpu.SemaphoreType.DMA((points // tile,)),
            ],
            cost_estimate=pl.CostEstimate(
                flops=2 * sources * points * rows * shots,
                bytes_accessed=2 * sources * points * rows + 2 * points * shots,
                transcendentals=0,
            ),
            compiler_params=pltpu.CompilerParams(vmem_limit_bytes=LIMIT),
        )(evaluate, kept, came, self.last if field is None else field)
        return out


def swapped(shard, axis, mask):
    return lax.ppermute(shard, axis, [(i, i ^ mask) for i in range(lax.axis_size(axis))])


def shards(coeffs, weights, evaluate):
    coeffs, weights, evaluate = coeffs[0, 0], weights[0, 0], evaluate[0]
    coeffs = pltpu.with_memory_space_constraint(coeffs, pltpu.HBM)
    weights = pltpu.with_memory_space_constraint(weights, pltpu.HBM)
    order = Order()
    half0, half1, early = order.local_levels(coeffs, weights)
    halves = (half0, half1)

    def level4(b0, facing):
        jobs = [((0, i), (1, i), (0, (b0 * 8 + i, 0))) for i in range(8)]
        return order.level([halves[b0], facing], [early], [jobs])[0]

    def level5(b0, x, far, after):
        jobs = [
            [((0, 4 * b1 + i), (1, 4 * (1 - b1) + i), (0, (b0 * 8 + 4 * b1 + i, 1))) for i in range(4)]
            for b1 in range(2)
        ]
        return order.level([x, far], [early], jobs, after=after)

    def level6(c, x, far):
        base = c[0] * 8 + c[1] * 4
        jobs = [
            [((0, 2 * b2 + b3), (1, 2 * b2 + b3), (0, (base + 2 * b2 + b3, 2))) for b3 in range(2)]
            for b2 in range(2)
        ]
        return order.level([x, far], [early], jobs)

    def level7(c, keep, came):
        q = 2 * c[1] + c[0]
        jobs = [((r1, b3), (1 - r1, b3), (r1, (b3 * 4 + q, 0))) for b3 in range(2) for r1 in range(2)]
        return order.level([keep, came], [keep78, got1], [jobs], paired=True)[0]

    def level8(c, x, far):
        q = 2 * c[1] + c[0]
        jobs = [
            [((0, 2 * b3 + r1), (1, 2 * b3 + r1), (r1, (b3 * 4 + q, 1))) for r1 in range(2)]
            for b3 in range(2)
        ]
        return order.level([x, far], [keep78, got1], jobs)

    def late(c, r2, r1, l):
        q = 2 * c[1] + c[0]
        return ((0, (q, l)), (1, (8 + q, l)), (2, (q, l)), (3, (q, l)))[2 * r2 + r1]

    def level9(c, keep, came):
        jobs = [((r2, r1), (1 - r2, r1), late(c, r2, r1, 0)) for r1 in range(2) for r2 in range(2)]
        return order.level([keep, came], [keep9, got1, got2, got3], [jobs], paired=True)[0]

    def level10(c, x, far):
        jobs = [
            ((0, 2 * r1 + r2), (1, 2 * r1 + r2), late(c, r2, r1, 1)) for r2 in range(2) for r1 in range(2)
        ]
        return order.level([x, far], [keep9, got1, got2, got3], [jobs])[0]

    P0, Q0, P1, Q1 = (0, 1), (0, 0), (1, 1), (1, 0)
    near, far, keep, send, came, spread, fields = {}, {}, {}, {}, {}, {}, []

    def do4(b0):
        facing = swapped(halves[b0], "tgt", 1)
        spread[b0] = level4(b0, facing)
        far[b0] = swapped(spread[b0], "src", 1)

    def do5(b0, after):
        near[b0, 0], near[b0, 1] = level5(b0, spread[b0], far[b0], after)
        for b1 in FIRST:
            far[b0, b1] = swapped(near[b0, b1], "tgt", 2)

    def do6(c):
        keep[c], send[c] = level6(c, near[c], far[c])
        came[c] = swapped(send[c], "src", 2)

    def do7(c):
        near[c] = level7(c, keep[c], came[c])
        far[c] = swapped(near[c], "tgt", 4)

    def do8(c):
        keep[c], send[c] = level8(c, near[c], far[c])
        came[c] = swapped(send[c], "src", 4)

    def do9(c):
        near[c] = level9(c, keep[c], came[c])
        far[c] = swapped(near[c], "tgt", 8)

    def do10(c):
        near[c] = level10(c, near[c], far[c])
        if c[1]:
            came[c] = swapped(near[c], "src", 1)

    def finish(b0):
        before = fields[-1] if fields else None
        fields.append(order.evaluated(evaluate, near[b0, 0], came[b0, 1], b0, before))

    keep78, keep9, send1, send2, send3 = order.split_weights(weights)
    got2, got3, got1 = swapped(send2, "src", 4), swapped(send3, "src", 6), swapped(send1, "src", 2)
    do4(0), do4(1)
    do5(0, ()), do5(1, (got1, got2, got3))
    for step, chunk in STEPS:
        {6: do6, 7: do7, 8: do8, 9: do9, 10: do10, 11: finish}[step](chunk)
    field = fields[-1]
    return field[None]


def solution(mesh):
    placed = (
        P("src", "tgt", None, None, None),
        P("src", "tgt", None, None, None, None),
        P("tgt", "src", None, None, None),
    )
    return jax.shard_map(
        shards, mesh=mesh, in_specs=placed, out_specs=P("tgt", "src", None, None), check_vma=False
    )
```

```python
import jax
import jax.numpy as jnp
from jax import lax
from jax.experimental import pallas as pl
from jax.experimental.pallas import tpu as pltpu
from jax.sharding import PartitionSpec as P

BF16 = jnp.bfloat16
LIMIT = 40 * 1024 * 1024
LOCAL = 4


def stacked(w):
    n = w.shape[0]
    parts = [w[:, i * n : (i + 1) * n] for i in range(4)]
    top = jnp.concatenate([parts[0], -parts[1], parts[2], -parts[3]], axis=1)
    low = jnp.concatenate([parts[1], parts[0], parts[3], parts[2]], axis=1)
    return jnp.concatenate([top, low], axis=0)


def combine(w, own, partner):
    both = jnp.concatenate([own, partner], axis=0)
    return jnp.dot(stacked(w), both, preferred_element_type=jnp.float32).astype(BF16)


def combine_pair(wa, wb, xa, xb):
    n = 2 * wa.shape[0]
    first, second = stacked(wa), stacked(wb)
    second = jnp.concatenate([second[:, n:], second[:, :n]], axis=1)
    lhs = jnp.concatenate([first, second], axis=0)
    out = jnp.dot(lhs, jnp.concatenate([xa, xb], axis=0), preferred_element_type=jnp.float32)
    out = out.astype(BF16)
    return out[:n], out[n:]


def call(body, out_shapes, args, specs=None, scratch=(), flops=0, moved=0):
    return pl.pallas_call(
        body,
        out_shape=[jax.ShapeDtypeStruct(s, BF16) for s in out_shapes],
        in_specs=specs or [pl.BlockSpec(memory_space=pltpu.VMEM)] * len(args),
        out_specs=[pl.BlockSpec(memory_space=pltpu.VMEM)] * len(out_shapes),
        scratch_shapes=list(scratch),
        cost_estimate=pl.CostEstimate(flops=0, bytes_accessed=1, transcendentals=0),
        compiler_params=pltpu.CompilerParams(vmem_limit_bytes=LIMIT),
    )(*args)


class Order:
    def __init__(self):
        self.last = None

    def level(self, arrays, weights, outs, paired=False, after=()):
        na, nw = len(arrays), len(weights)
        rows, shots = arrays[0].shape[1:]

        def body(*refs):
            x, w, o = refs[:na], refs[na : na + nw], refs[len(args) :]
            get = lambda refs, at: refs[at[0]][at[1]]
            for k, jobs in enumerate(outs):
                if paired:
                    for i in range(0, len(jobs), 2):
                        (xa, xb, wa), (_, _, wb) = jobs[i], jobs[i + 1]
                        o[k][i], o[k][i + 1] = combine_pair(get(w, wa), get(w, wb), get(x, xa), get(x, xb))
                else:
                    for i, (xa, xb, wa) in enumerate(jobs):
                        o[k][i] = combine(get(w, wa), get(x, xa), get(x, xb))

        args = list(arrays) + list(weights) + list(after)
        if self.last is not None:
            args.append(self.last)
        jobs = sum(len(j) for j in outs)
        results = call(
            body,
            [(len(j), rows, shots) for j in outs],
            args,
            flops=2 * jobs * rows * 2 * rows * shots,
            moved=jobs * rows * shots * 4,
        )
        self.last = results[0]
        return results

    def split(self, weights, plan, boxes):
        rank, cols = weights.shape[2:]

        def body(w, _, *refs):
            outs, sems = refs[:-1], refs[-1]
            flip = lax.axis_index("src") * 2
            copies = []
            for i, ((b0, b1, b2, b3), first, k, at) in enumerate(plan):
                box = jnp.bitwise_xor(b0 + 2 * b1 + 4 * b2 + 8 * b3, flip)
                copies.append(pltpu.make_async_copy(w.at[box, pl.ds(first, 2)], outs[k].at[at], sems.at[i]))
            for c in copies:
                c.start()
            for c in copies:
                c.wait()

        results = call(
            body,
            [(n, 2, rank, cols) for n in boxes],
            [weights, self.last],
            specs=[pl.BlockSpec(memory_space=pltpu.HBM), pl.BlockSpec(memory_space=pltpu.VMEM)],
            scratch=[pltpu.SemaphoreType.DMA((len(plan),))],
            moved=1,
        )
        self.last = results[0]
        return results

    def local_levels(self, coeffs, weights):
        loc, rows, shots = coeffs.shape
        rank, cols = weights.shape[2:]

        def body(x_hbm, w, out0, out1, early, x, wbuf, buf, sem, sems, early_sems):
            flip = lax.axis_index("src") * 2

            def actual(r):
                b0, b1, b2, b3 = r >> 3, (r >> 2) & 1, (r >> 1) & 1, r & 1
                return jnp.bitwise_xor(b0 + 2 * b1 + 4 * b2 + 8 * b3, flip)

            fetch = pltpu.make_async_copy(x_hbm, x, sem)
            fetch.start()
            copies = [
                pltpu.make_async_copy(w.at[:, l], wbuf.at[l], sems.at[l]) for l in range(LOCAL)
            ]
            copies[0].start()
            later = [
                pltpu.make_async_copy(w.at[actual(r), pl.ds(LOCAL, 3)], early.at[r], early_sems.at[r])
                for r in range(loc)
            ]
            fetch.wait()
            for l in range(LOCAL):
                copies[l].wait()
                if l == 0:
                    for c in copies[1:] + later:
                        c.start()
                src = x if l == 0 else buf.at[(l - 1) % 2]
                dst = buf.at[l % 2]
                if l < LOCAL - 1:
                    for b in range(loc):
                        far = b ^ (1 << l)
                        if b < far:
                            dst[b], dst[far] = combine_pair(wbuf[l, b], wbuf[l, far], src[b], src[far])
                else:
                    for r in range(0, loc, 2):
                        b, far = actual(r), actual(r + 1)
                        out = out1 if r >= loc // 2 else out0
                        i = r % (loc // 2)
                        out[i], out[i + 1] = combine_pair(wbuf[l, b], wbuf[l, far], src[b], src[far])
            for c in later:
                c.wait()

        results = call(
            body,
            [(loc // 2, rows, shots)] * 2 + [(loc, 3, rank, cols)],
            [coeffs, weights],
            specs=[pl.BlockSpec(memory_space=pltpu.HBM)] * 2,
            scratch=[
                pltpu.VMEM((loc, rows, shots), BF16),
                pltpu.VMEM((LOCAL, loc, rank, cols), BF16),
                pltpu.VMEM((2, loc, rows, shots), BF16),
                pltpu.SemaphoreType.DMA,
                pltpu.SemaphoreType.DMA((LOCAL,)),
                pltpu.SemaphoreType.DMA((loc,)),
            ],
            flops=2 * LOCAL * loc * rows * 2 * rows * shots,
            moved=LOCAL * loc * rank * cols * 2,
        )
        self.last = results[0]
        return results

    def evaluated(self, evaluate, kept, came, box, field):
        boxes, sources, points, rows = evaluate.shape
        shots = kept.shape[2]
        tile = 256

        def body(e, k, c, _, out, buf, sems):
            me = lax.axis_index("src")
            copies = []
            for i in range(points // tile):
                rng = slice(i * tile, (i + 1) * tile)
                total = jnp.zeros((tile, shots), jnp.float32)
                for pair in range(sources // 2):
                    b2, b1 = pair >> 1, pair & 1
                    near = jnp.bitwise_xor(me, 2 * b1 + 4 * b2)
                    far = jnp.bitwise_xor(near, 1)
                    lhs = jnp.concatenate([e[box, near, rng], e[box, far, rng]], axis=1)
                    rhs = jnp.concatenate([k[pair], c[pair]], axis=0)
                    total += jnp.dot(lhs, rhs, preferred_element_type=jnp.float32)
                buf[i] = total.astype(BF16)
                copies.append(pltpu.make_async_copy(buf.at[i], out.at[box, pl.ds(i * tile, tile)], sems.at[i]))
                copies[-1].start()
            for copy in copies:
                copy.wait()

        vmem = pl.BlockSpec(memory_space=pltpu.VMEM)
        hbm = pl.BlockSpec(memory_space=pltpu.HBM)
        out = pl.pallas_call(
            body,
            out_shape=jax.ShapeDtypeStruct((boxes, points, shots), BF16),
            in_specs=[vmem, vmem, vmem, vmem if field is None else hbm],
            out_specs=hbm,
            input_output_aliases={} if field is None else {3: 0},
            scratch_shapes=[
                pltpu.VMEM((points // tile, tile, shots), BF16),
                pltpu.SemaphoreType.DMA((points // tile,)),
            ],
            cost_estimate=pl.CostEstimate(
                flops=2 * sources * points * rows * shots,
                bytes_accessed=2 * sources * points * rows + 2 * points * shots,
                transcendentals=0,
            ),
            compiler_params=pltpu.CompilerParams(vmem_limit_bytes=LIMIT),
        )(evaluate, kept, came, self.last if field is None else field)
        return out


def swapped(shard, axis, mask):
    return lax.ppermute(shard, axis, [(i, i ^ mask) for i in range(lax.axis_size(axis))])


def shards(coeffs, weights, evaluate):
    coeffs, weights, evaluate = coeffs[0, 0], weights[0, 0], evaluate[0]
    coeffs = pltpu.with_memory_space_constraint(coeffs, pltpu.HBM)
    weights = pltpu.with_memory_space_constraint(weights, pltpu.HBM)
    order = Order()
    half0, half1, early = order.local_levels(coeffs, weights)
    halves = (half0, half1)

    def level4(b0, facing):
        jobs = [((0, i), (1, i), (0, (b0 * 8 + i, 0))) for i in range(8)]
        return order.level([halves[b0], facing], [early], [jobs])[0]

    def level5(b0, x, far, after):
        jobs = [
            [((0, 4 * b1 + i), (1, 4 * (1 - b1) + i), (0, (b0 * 8 + 4 * b1 + i, 1))) for i in range(4)]
            for b1 in range(2)
        ]
        return order.level([x, far], [early], jobs, after=after)

    def level6(c, x, far, after):
        base = c[0] * 8 + c[1] * 4
        jobs = [
            [((0, 2 * b2 + b3), (1, 2 * b2 + b3), (0, (base + 2 * b2 + b3, 2))) for b3 in range(2)]
            for b2 in range(2)
        ]
        return order.level([x, far], [early], jobs, after=after)

    def level7(c, keep, came, after):
        q = 2 * c[1] + c[0]
        jobs = [((r1, b3), (1 - r1, b3), (r1, (b3 * 4 + q, 0))) for b3 in range(2) for r1 in range(2)]
        return order.level([keep, came], [keep78, got1], [jobs], paired=True, after=after)[0]

    def level8(c, x, far):
        q = 2 * c[1] + c[0]
        jobs = [
            [((0, 2 * b3 + r1), (1, 2 * b3 + r1), (r1, (b3 * 4 + q, 1))) for r1 in range(2)]
            for b3 in range(2)
        ]
        return order.level([x, far], [keep78, got1], jobs)

    def late(c, r2, r1, l):
        q = 2 * c[1] + c[0]
        return ((0, (q, l)), (1, (8 + q, l)), (2, (q, l)), (3, (q, l)))[2 * r2 + r1]

    def level9(c, keep, came, after):
        jobs = [((r2, r1), (1 - r2, r1), late(c, r2, r1, 0)) for r1 in range(2) for r2 in range(2)]
        return order.level([keep, came], [keep9, got1, got2, got3], [jobs], paired=True, after=after)[0]

    def level10(c, x, far):
        jobs = [
            ((0, 2 * r1 + r2), (1, 2 * r1 + r2), late(c, r2, r1, 1)) for r2 in range(2) for r1 in range(2)
        ]
        return order.level([x, far], [keep9, got1, got2, got3], [jobs])[0]

    P0, Q0, P1, Q1 = (0, 1), (0, 0), (1, 1), (1, 0)
    near, far, keep, send, came, spread, fields = {}, {}, {}, {}, {}, {}, []

    facing = [swapped(h, "tgt", 1) for h in halves]

    def do4(b0):
        spread[b0] = level4(b0, facing[b0])
        far[b0] = swapped(spread[b0], "src", 1)

    def do5(b0, after):
        near[b0, 0], near[b0, 1] = level5(b0, spread[b0], far[b0], after)
        for b1 in (1, 0):
            far[b0, b1] = swapped(near[b0, b1], "tgt", 2)

    def do6(c, after=()):
        keep[c], send[c] = level6(c, near[c], far[c], after)
        came[c] = swapped(send[c], "src", 2)

    def do7(c, after=()):
        near[c] = level7(c, keep[c], came[c], after)
        far[c] = swapped(near[c], "tgt", 4)

    def do8(c):
        keep[c], send[c] = level8(c, near[c], far[c])
        came[c] = swapped(send[c], "src", 4)

    def do9(c, after=()):
        near[c] = level9(c, keep[c], came[c], after)
        far[c] = swapped(near[c], "tgt", 8)

    def do10(c):
        near[c] = level10(c, near[c], far[c])
        if c[1]:
            came[c] = swapped(near[c], "src", 1)

    def finish(b0):
        before = fields[-1] if fields else None
        fields.append(order.evaluated(evaluate, near[b0, 0], came[b0, 1], b0, before))

    two, quads = (0, 1), [(q & 1, q >> 1) for q in range(4)]
    plan = [((b0, b1, b2, 1), 9, b2, 2 * b1 + b0) for b0, b1 in quads for b2 in two]
    send2, send3 = order.split(weights, plan, (4, 4))
    do4(0), do4(1)
    plan = [((b0, b1, b2, b3), 7, b2, b3 * 4 + 2 * b1 + b0) for b2 in two for b3 in two for b0, b1 in quads]
    plan += [((b0, b1, 1, 0), 9, 1, 8 + 2 * b1 + b0) for b0, b1 in quads]
    plan += [((b0, b1, 0, 0), 9, 2, 2 * b1 + b0) for b0, b1 in quads]
    keep78, send1, keep9 = order.split(weights, plan, (8, 12, 4))
    got1, got2, got3 = swapped(send1, "src", 2), swapped(send2, "src", 4), swapped(send3, "src", 6)
    do5(0, ()), do5(1, ())
    do6(P0, (got1,)), do7(P0, (got2, got3)), do6(P1), do6(Q0), do7(P1), do7(Q0), do6(Q1), do8(P0)
    do9(P0), do8(P1), do7(Q1), do8(Q0), do9(P1), do10(P0), do9(Q0), do8(Q1)
    do10(P1), do9(Q1), do10(Q0), finish(0), do10(Q1), finish(1)
    field = fields[-1]
    return field[None]


def solution(mesh):
    placed = (
        P("src", "tgt", None, None, None),
        P("src", "tgt", None, None, None, None),
        P("tgt", "src", None, None, None),
    )
    return jax.shard_map(
        shards, mesh=mesh, in_specs=placed, out_specs=P("tgt", "src", None, None), check_vma=False
    )
```

```python
import jax
import jax.numpy as jnp
from jax import lax
from jax.experimental import pallas as pl
from jax.experimental.pallas import tpu as pltpu
from jax.sharding import PartitionSpec as P

BF16 = jnp.bfloat16
LIMIT = 40 * 1024 * 1024
LOCAL = 4


def stacked(w):
    n = w.shape[0]
    parts = [w[:, i * n : (i + 1) * n] for i in range(4)]
    top = jnp.concatenate([parts[0], -parts[1], parts[2], -parts[3]], axis=1)
    low = jnp.concatenate([parts[1], parts[0], parts[3], parts[2]], axis=1)
    return jnp.concatenate([top, low], axis=0)


def combine(w, own, partner):
    both = jnp.concatenate([own, partner], axis=0)
    return jnp.dot(stacked(w), both, preferred_element_type=jnp.float32).astype(BF16)


def combine_pair(wa, wb, xa, xb):
    n = 2 * wa.shape[0]
    first, second = stacked(wa), stacked(wb)
    second = jnp.concatenate([second[:, n:], second[:, :n]], axis=1)
    lhs = jnp.concatenate([first, second], axis=0)
    out = jnp.dot(lhs, jnp.concatenate([xa, xb], axis=0), preferred_element_type=jnp.float32)
    out = out.astype(BF16)
    return out[:n], out[n:]


def call(body, out_shapes, args, specs=None, scratch=(), flops=0, moved=0):
    return pl.pallas_call(
        body,
        out_shape=[jax.ShapeDtypeStruct(s, BF16) for s in out_shapes],
        in_specs=specs or [pl.BlockSpec(memory_space=pltpu.VMEM)] * len(args),
        out_specs=[pl.BlockSpec(memory_space=pltpu.VMEM)] * len(out_shapes),
        scratch_shapes=list(scratch),
        cost_estimate=pl.CostEstimate(flops=0, bytes_accessed=1, transcendentals=0),
        compiler_params=pltpu.CompilerParams(vmem_limit_bytes=LIMIT),
    )(*args)


class Order:
    def __init__(self):
        self.last = None

    def level(self, arrays, weights, outs, paired=False, after=()):
        na, nw = len(arrays), len(weights)
        rows, shots = arrays[0].shape[1:]

        def body(*refs):
            x, w, o = refs[:na], refs[na : na + nw], refs[len(args) :]
            flip = lax.axis_index("src") * 2

            def get(refs, at):
                if len(at) == 2:
                    return refs[at[0]][at[1]]
                return refs[at[0]][jnp.bitwise_xor(at[1], flip), at[2]]

            for k, jobs in enumerate(outs):
                if paired:
                    for i in range(0, len(jobs), 2):
                        (xa, xb, wa), (_, _, wb) = jobs[i], jobs[i + 1]
                        o[k][i], o[k][i + 1] = combine_pair(get(w, wa), get(w, wb), get(x, xa), get(x, xb))
                else:
                    for i, (xa, xb, wa) in enumerate(jobs):
                        o[k][i] = combine(get(w, wa), get(x, xa), get(x, xb))

        args = list(arrays) + list(weights) + list(after)
        if self.last is not None:
            args.append(self.last)
        jobs = sum(len(j) for j in outs)
        results = call(
            body,
            [(len(j), rows, shots) for j in outs],
            args,
            flops=2 * jobs * rows * 2 * rows * shots,
            moved=jobs * rows * shots * 4,
        )
        self.last = results[0]
        return results

    def split(self, weights, plan, boxes):
        rank, cols = weights.shape[2:]

        def body(w, _, *refs):
            outs, sems = refs[:-1], refs[-1]
            flip = lax.axis_index("src") * 2
            copies = []
            for i, ((b0, b1, b2, b3), first, k, at) in enumerate(plan):
                box = jnp.bitwise_xor(b0 + 2 * b1 + 4 * b2 + 8 * b3, flip)
                copies.append(pltpu.make_async_copy(w.at[box, pl.ds(first, 2)], outs[k].at[at], sems.at[i]))
            for c in copies:
                c.start()
            for c in copies:
                c.wait()

        results = call(
            body,
            [(n, 2, rank, cols) for n in boxes],
            [weights, self.last],
            specs=[pl.BlockSpec(memory_space=pltpu.HBM), pl.BlockSpec(memory_space=pltpu.VMEM)],
            scratch=[pltpu.SemaphoreType.DMA((len(plan),))],
            moved=1,
        )
        self.last = results[0]
        return results

    def local_levels(self, coeffs, weights):
        loc, rows, shots = coeffs.shape
        rank, cols = weights.shape[2:]

        def body(x_hbm, w, out0, out1, early, x, wbuf, buf, sem, sems, early_sem):
            flip = lax.axis_index("src") * 2

            def actual(r):
                b0, b1, b2, b3 = r >> 3, (r >> 2) & 1, (r >> 1) & 1, r & 1
                return jnp.bitwise_xor(b0 + 2 * b1 + 4 * b2 + 8 * b3, flip)

            fetch = pltpu.make_async_copy(x_hbm, x, sem)
            fetch.start()
            copies = [
                pltpu.make_async_copy(w.at[:, l], wbuf.at[l], sems.at[l]) for l in range(LOCAL)
            ]
            copies[0].start()
            later = [pltpu.make_async_copy(w.at[:, pl.ds(LOCAL, 3)], early, early_sem)]
            fetch.wait()
            for l in range(LOCAL):
                copies[l].wait()
                if l == 0:
                    for c in copies[1:] + later:
                        c.start()
                src = x if l == 0 else buf.at[(l - 1) % 2]
                dst = buf.at[l % 2]
                if l < LOCAL - 1:
                    for b in range(loc):
                        far = b ^ (1 << l)
                        if b < far:
                            dst[b], dst[far] = combine_pair(wbuf[l, b], wbuf[l, far], src[b], src[far])
                else:
                    for r in range(0, loc, 2):
                        b, far = actual(r), actual(r + 1)
                        out = out1 if r >= loc // 2 else out0
                        i = r % (loc // 2)
                        out[i], out[i + 1] = combine_pair(wbuf[l, b], wbuf[l, far], src[b], src[far])
            for c in later:
                c.wait()

        results = call(
            body,
            [(loc // 2, rows, shots)] * 2 + [(loc, 3, rank, cols)],
            [coeffs, weights],
            specs=[pl.BlockSpec(memory_space=pltpu.HBM)] * 2,
            scratch=[
                pltpu.VMEM((loc, rows, shots), BF16),
                pltpu.VMEM((LOCAL, loc, rank, cols), BF16),
                pltpu.VMEM((2, loc, rows, shots), BF16),
                pltpu.SemaphoreType.DMA,
                pltpu.SemaphoreType.DMA((LOCAL,)),
                pltpu.SemaphoreType.DMA,
            ],
            flops=2 * LOCAL * loc * rows * 2 * rows * shots,
            moved=LOCAL * loc * rank * cols * 2,
        )
        self.last = results[0]
        return results

    def evaluated(self, evaluate, kept, came, box, field):
        boxes, sources, points, rows = evaluate.shape
        shots = kept.shape[2]
        tile = 256

        def body(e, k, c, _, out, buf, sems):
            me = lax.axis_index("src")
            copies = []
            for i in range(points // tile):
                rng = slice(i * tile, (i + 1) * tile)
                total = jnp.zeros((tile, shots), jnp.float32)
                for pair in range(sources // 2):
                    b2, b1 = pair >> 1, pair & 1
                    near = jnp.bitwise_xor(me, 2 * b1 + 4 * b2)
                    far = jnp.bitwise_xor(near, 1)
                    lhs = jnp.concatenate([e[box, near, rng], e[box, far, rng]], axis=1)
                    rhs = jnp.concatenate([k[pair], c[pair]], axis=0)
                    total += jnp.dot(lhs, rhs, preferred_element_type=jnp.float32)
                buf[i] = total.astype(BF16)
                copies.append(pltpu.make_async_copy(buf.at[i], out.at[box, pl.ds(i * tile, tile)], sems.at[i]))
                copies[-1].start()
            for copy in copies:
                copy.wait()

        vmem = pl.BlockSpec(memory_space=pltpu.VMEM)
        hbm = pl.BlockSpec(memory_space=pltpu.HBM)
        out = pl.pallas_call(
            body,
            out_shape=jax.ShapeDtypeStruct((boxes, points, shots), BF16),
            in_specs=[vmem, vmem, vmem, vmem if field is None else hbm],
            out_specs=hbm,
            input_output_aliases={} if field is None else {3: 0},
            scratch_shapes=[
                pltpu.VMEM((points // tile, tile, shots), BF16),
                pltpu.SemaphoreType.DMA((points // tile,)),
            ],
            cost_estimate=pl.CostEstimate(
                flops=2 * sources * points * rows * shots,
                bytes_accessed=2 * sources * points * rows + 2 * points * shots,
                transcendentals=0,
            ),
            compiler_params=pltpu.CompilerParams(vmem_limit_bytes=LIMIT),
        )(evaluate, kept, came, self.last if field is None else field)
        return out


def swapped(shard, axis, mask):
    return lax.ppermute(shard, axis, [(i, i ^ mask) for i in range(lax.axis_size(axis))])


def shards(coeffs, weights, evaluate):
    coeffs, weights, evaluate = coeffs[0, 0], weights[0, 0], evaluate[0]
    coeffs = pltpu.with_memory_space_constraint(coeffs, pltpu.HBM)
    weights = pltpu.with_memory_space_constraint(weights, pltpu.HBM)
    order = Order()
    half0, half1, early = order.local_levels(coeffs, weights)
    halves = (half0, half1)

    def box(b0, b1, b2, b3):
        return b0 + 2 * b1 + 4 * b2 + 8 * b3

    def level4(b0, facing):
        jobs = [((0, i), (1, i), (0, box(b0, i >> 2, (i >> 1) & 1, i & 1), 0)) for i in range(8)]
        return order.level([halves[b0], facing], [early], [jobs])[0]

    def level5(b0, x, far, after):
        jobs = [
            [((0, 4 * b1 + i), (1, 4 * (1 - b1) + i), (0, box(b0, b1, i >> 1, i & 1), 1)) for i in range(4)]
            for b1 in range(2)
        ]
        return order.level([x, far], [early], jobs, after=after)

    def level6(c, x, far, after):
        jobs = [
            [((0, 2 * b2 + b3), (1, 2 * b2 + b3), (0, box(c[0], c[1], b2, b3), 2)) for b3 in range(2)]
            for b2 in range(2)
        ]
        return order.level([x, far], [early], jobs, after=after)

    def level7(c, keep, came, after):
        q = 2 * c[1] + c[0]
        jobs = [((r1, b3), (1 - r1, b3), (r1, (b3 * 4 + q, 0))) for b3 in range(2) for r1 in range(2)]
        return order.level([keep, came], [keep78, got1], [jobs], paired=True, after=after)[0]

    def level8(c, x, far):
        q = 2 * c[1] + c[0]
        jobs = [
            [((0, 2 * b3 + r1), (1, 2 * b3 + r1), (r1, (b3 * 4 + q, 1))) for r1 in range(2)]
            for b3 in range(2)
        ]
        return order.level([x, far], [keep78, got1], jobs)

    def late(c, r2, r1, l):
        q = 2 * c[1] + c[0]
        return ((0, (q, l)), (1, (8 + q, l)), (2, (q, l)), (3, (q, l)))[2 * r2 + r1]

    def level9(c, keep, came, after):
        jobs = [((r2, r1), (1 - r2, r1), late(c, r2, r1, 0)) for r1 in range(2) for r2 in range(2)]
        return order.level([keep, came], [keep9, got1, got2, got3], [jobs], paired=True, after=after)[0]

    def level10(c, x, far):
        jobs = [
            ((0, 2 * r1 + r2), (1, 2 * r1 + r2), late(c, r2, r1, 1)) for r2 in range(2) for r1 in range(2)
        ]
        return order.level([x, far], [keep9, got1, got2, got3], [jobs])[0]

    P0, Q0, P1, Q1 = (0, 1), (0, 0), (1, 1), (1, 0)
    near, far, keep, send, came, spread, fields = {}, {}, {}, {}, {}, {}, []

    facing = [swapped(h, "tgt", 1) for h in halves]

    def do4(b0):
        spread[b0] = level4(b0, facing[b0])
        far[b0] = swapped(spread[b0], "src", 1)

    def do5(b0, after):
        near[b0, 0], near[b0, 1] = level5(b0, spread[b0], far[b0], after)
        for b1 in (1, 0):
            far[b0, b1] = swapped(near[b0, b1], "tgt", 2)

    def do6(c, after=()):
        keep[c], send[c] = level6(c, near[c], far[c], after)
        came[c] = swapped(send[c], "src", 2)

    def do7(c, after=()):
        near[c] = level7(c, keep[c], came[c], after)
        far[c] = swapped(near[c], "tgt", 4)

    def do8(c):
        keep[c], send[c] = level8(c, near[c], far[c])
        came[c] = swapped(send[c], "src", 4)

    def do9(c, after=()):
        near[c] = level9(c, keep[c], came[c], after)
        far[c] = swapped(near[c], "tgt", 8)

    def do10(c):
        near[c] = level10(c, near[c], far[c])
        if c[1]:
            came[c] = swapped(near[c], "src", 1)

    def finish(b0):
        before = fields[-1] if fields else None
        fields.append(order.evaluated(evaluate, near[b0, 0], came[b0, 1], b0, before))

    two, quads = (0, 1), [(q & 1, q >> 1) for q in range(4)]
    plan = [((b0, b1, b2, 1), 9, b2, 2 * b1 + b0) for b0, b1 in quads for b2 in two]
    send2, send3 = order.split(weights, plan, (4, 4))
    do4(0), do4(1)
    plan = [((b0, b1, b2, b3), 7, b2, b3 * 4 + 2 * b1 + b0) for b2 in two for b3 in two for b0, b1 in quads]
    plan += [((b0, b1, 1, 0), 9, 1, 8 + 2 * b1 + b0) for b0, b1 in quads]
    plan += [((b0, b1, 0, 0), 9, 2, 2 * b1 + b0) for b0, b1 in quads]
    keep78, send1, keep9 = order.split(weights, plan, (8, 12, 4))
    got1, got2, got3 = swapped(send1, "src", 2), swapped(send2, "src", 4), swapped(send3, "src", 6)
    do5(0, ()), do5(1, ())
    do6(P0, (got1,)), do7(P0, (got2, got3)), do6(P1), do6(Q0), do7(P1), do8(P0), do7(Q0), do6(Q1)
    do9(P0), do8(P1), do7(Q1), do8(Q0), do9(P1), do9(Q0), do10(P0), do8(Q1)
    do10(P1), do9(Q1), do10(Q0), finish(0), do10(Q1), finish(1)
    field = fields[-1]
    return field[None]


def solution(mesh):
    placed = (
        P("src", "tgt", None, None, None),
        P("src", "tgt", None, None, None, None),
        P("tgt", "src", None, None, None),
    )
    return jax.shard_map(
        shards, mesh=mesh, in_specs=placed, out_specs=P("tgt", "src", None, None), check_vma=False
    )
```

```python
import jax
import jax.numpy as jnp
from jax import lax
from jax.experimental import pallas as pl
from jax.experimental.pallas import tpu as pltpu
from jax.sharding import PartitionSpec as P

BF16 = jnp.bfloat16
LIMIT = 40 * 1024 * 1024
LOCAL = 4


def stacked(w):
    n = w.shape[0]
    parts = [w[:, i * n : (i + 1) * n] for i in range(4)]
    top = jnp.concatenate([parts[0], -parts[1], parts[2], -parts[3]], axis=1)
    low = jnp.concatenate([parts[1], parts[0], parts[3], parts[2]], axis=1)
    return jnp.concatenate([top, low], axis=0)


def combine(w, own, partner):
    both = jnp.concatenate([own, partner], axis=0)
    return jnp.dot(stacked(w), both, preferred_element_type=jnp.float32).astype(BF16)


def combine_pair(wa, wb, xa, xb):
    n = 2 * wa.shape[0]
    first, second = stacked(wa), stacked(wb)
    second = jnp.concatenate([second[:, n:], second[:, :n]], axis=1)
    lhs = jnp.concatenate([first, second], axis=0)
    out = jnp.dot(lhs, jnp.concatenate([xa, xb], axis=0), preferred_element_type=jnp.float32)
    out = out.astype(BF16)
    return out[:n], out[n:]


def call(body, out_shapes, args, specs=None, scratch=(), flops=0, moved=0):
    return pl.pallas_call(
        body,
        out_shape=[jax.ShapeDtypeStruct(s, BF16) for s in out_shapes],
        in_specs=specs or [pl.BlockSpec(memory_space=pltpu.VMEM)] * len(args),
        out_specs=[pl.BlockSpec(memory_space=pltpu.VMEM)] * len(out_shapes),
        scratch_shapes=list(scratch),
        cost_estimate=pl.CostEstimate(flops=0, bytes_accessed=1, transcendentals=0),
        compiler_params=pltpu.CompilerParams(vmem_limit_bytes=LIMIT),
    )(*args)


class Order:
    def __init__(self):
        self.last = None

    def level(self, arrays, weights, outs, paired=False, after=()):
        na, nw = len(arrays), len(weights)
        rows, shots = arrays[0].shape[1:]

        def body(*refs):
            x, w, o = refs[:na], refs[na : na + nw], refs[len(args) :]
            flip = lax.axis_index("src") * 2

            def get(refs, at):
                if len(at) == 2:
                    return refs[at[0]][at[1]]
                return refs[at[0]][jnp.bitwise_xor(at[1], flip), at[2]]

            for k, jobs in enumerate(outs):
                if paired:
                    for i in range(0, len(jobs), 2):
                        (xa, xb, wa), (_, _, wb) = jobs[i], jobs[i + 1]
                        o[k][i], o[k][i + 1] = combine_pair(get(w, wa), get(w, wb), get(x, xa), get(x, xb))
                else:
                    for i, (xa, xb, wa) in enumerate(jobs):
                        o[k][i] = combine(get(w, wa), get(x, xa), get(x, xb))

        args = list(arrays) + list(weights) + list(after)
        if self.last is not None:
            args.append(self.last)
        jobs = sum(len(j) for j in outs)
        results = call(
            body,
            [(len(j), rows, shots) for j in outs],
            args,
            flops=2 * jobs * rows * 2 * rows * shots,
            moved=jobs * rows * shots * 4,
        )
        self.last = results[0]
        return results

    def split(self, weights, plan, boxes):
        rank, cols = weights.shape[2:]

        def body(w, _, *refs):
            outs, sems = refs[:-1], refs[-1]
            flip = lax.axis_index("src") * 2
            copies = []
            for i, ((b0, b1, b2, b3), first, k, at) in enumerate(plan):
                box = jnp.bitwise_xor(b0 + 2 * b1 + 4 * b2 + 8 * b3, flip)
                copies.append(pltpu.make_async_copy(w.at[box, pl.ds(first, 2)], outs[k].at[at], sems.at[i]))
            for c in copies:
                c.start()
            for c in copies:
                c.wait()

        results = call(
            body,
            [(n, 2, rank, cols) for n in boxes],
            [weights, self.last],
            specs=[pl.BlockSpec(memory_space=pltpu.HBM), pl.BlockSpec(memory_space=pltpu.VMEM)],
            scratch=[pltpu.SemaphoreType.DMA((len(plan),))],
            moved=1,
        )
        self.last = results[0]
        return results

    def local_levels(self, coeffs, weights):
        loc, rows, shots = coeffs.shape
        rank, cols = weights.shape[2:]

        def body(x_hbm, w, out0, out1, early, x, wbuf, buf, sem, sems, early_sem):
            flip = lax.axis_index("src") * 2

            def actual(r):
                b0, b1, b2, b3 = r >> 3, (r >> 2) & 1, (r >> 1) & 1, r & 1
                return jnp.bitwise_xor(b0 + 2 * b1 + 4 * b2 + 8 * b3, flip)

            fetch = pltpu.make_async_copy(x_hbm, x, sem)
            fetch.start()
            copies = [
                pltpu.make_async_copy(w.at[:, l], wbuf.at[l], sems.at[l]) for l in range(LOCAL)
            ]
            copies[0].start()
            later = [pltpu.make_async_copy(w.at[:, pl.ds(LOCAL, 3)], early, early_sem)]
            fetch.wait()
            for l in range(LOCAL):
                copies[l].wait()
                if l == 0:
                    for c in copies[1:] + later:
                        c.start()
                src = x if l == 0 else buf.at[(l - 1) % 2]
                dst = buf.at[l % 2]
                if l < LOCAL - 1:
                    for b in range(loc):
                        far = b ^ (1 << l)
                        if b < far:
                            dst[b], dst[far] = combine_pair(wbuf[l, b], wbuf[l, far], src[b], src[far])
                else:
                    for r in range(0, loc, 2):
                        b, far = actual(r), actual(r + 1)
                        out = out1 if r >= loc // 2 else out0
                        i = r % (loc // 2)
                        out[i], out[i + 1] = combine_pair(wbuf[l, b], wbuf[l, far], src[b], src[far])
            for c in later:
                c.wait()

        results = call(
            body,
            [(loc // 2, rows, shots)] * 2 + [(loc, 3, rank, cols)],
            [coeffs, weights],
            specs=[pl.BlockSpec(memory_space=pltpu.HBM)] * 2,
            scratch=[
                pltpu.VMEM((loc, rows, shots), BF16),
                pltpu.VMEM((LOCAL, loc, rank, cols), BF16),
                pltpu.VMEM((2, loc, rows, shots), BF16),
                pltpu.SemaphoreType.DMA,
                pltpu.SemaphoreType.DMA((LOCAL,)),
                pltpu.SemaphoreType.DMA,
            ],
            flops=2 * LOCAL * loc * rows * 2 * rows * shots,
            moved=LOCAL * loc * rank * cols * 2,
        )
        self.last = results[0]
        return results

    def evaluated(self, evaluate, kept, came, box, field):
        boxes, sources, points, rows = evaluate.shape
        shots = kept.shape[2]
        tile = 256

        def body(e, k, c, _, out, buf, sems):
            me = lax.axis_index("src")
            copies = []
            for i in range(points // tile):
                rng = slice(i * tile, (i + 1) * tile)
                total = jnp.zeros((tile, shots), jnp.float32)
                for pair in range(sources // 2):
                    b2, b1 = pair >> 1, pair & 1
                    near = jnp.bitwise_xor(me, 2 * b1 + 4 * b2)
                    far = jnp.bitwise_xor(near, 1)
                    lhs = jnp.concatenate([e[box, near, rng], e[box, far, rng]], axis=1)
                    rhs = jnp.concatenate([k[pair], c[pair]], axis=0)
                    total += jnp.dot(lhs, rhs, preferred_element_type=jnp.float32)
                buf[i] = total.astype(BF16)
                copies.append(pltpu.make_async_copy(buf.at[i], out.at[box, pl.ds(i * tile, tile)], sems.at[i]))
                copies[-1].start()
            for copy in copies:
                copy.wait()

        vmem = pl.BlockSpec(memory_space=pltpu.VMEM)
        hbm = pl.BlockSpec(memory_space=pltpu.HBM)
        out = pl.pallas_call(
            body,
            out_shape=jax.ShapeDtypeStruct((boxes, points, shots), BF16),
            in_specs=[vmem, vmem, vmem, vmem if field is None else hbm],
            out_specs=hbm,
            input_output_aliases={} if field is None else {3: 0},
            scratch_shapes=[
                pltpu.VMEM((points // tile, tile, shots), BF16),
                pltpu.SemaphoreType.DMA((points // tile,)),
            ],
            cost_estimate=pl.CostEstimate(
                flops=2 * sources * points * rows * shots,
                bytes_accessed=2 * sources * points * rows + 2 * points * shots,
                transcendentals=0,
            ),
            compiler_params=pltpu.CompilerParams(vmem_limit_bytes=LIMIT),
        )(evaluate, kept, came, self.last if field is None else field)
        return out


def swapped(shard, axis, mask):
    return lax.ppermute(shard, axis, [(i, i ^ mask) for i in range(lax.axis_size(axis))])


def shards(coeffs, weights, evaluate):
    coeffs, weights, evaluate = coeffs[0, 0], weights[0, 0], evaluate[0]
    coeffs = pltpu.with_memory_space_constraint(coeffs, pltpu.HBM)
    weights = pltpu.with_memory_space_constraint(weights, pltpu.HBM)
    order = Order()
    half0, half1, early = order.local_levels(coeffs, weights)
    halves = (half0, half1)

    def box(b0, b1, b2, b3):
        return b0 + 2 * b1 + 4 * b2 + 8 * b3

    def level4(b0, facing):
        jobs = [((0, i), (1, i), (0, box(b0, i >> 2, (i >> 1) & 1, i & 1), 0)) for i in range(8)]
        return order.level([halves[b0], facing], [early], [jobs])[0]

    def level5(b0, x, far, after):
        jobs = [
            [((0, 4 * b1 + i), (1, 4 * (1 - b1) + i), (0, box(b0, b1, i >> 1, i & 1), 1)) for i in range(4)]
            for b1 in range(2)
        ]
        return order.level([x, far], [early], jobs, after=after)

    def level6(c, x, far, after):
        jobs = [
            [((0, 2 * b2 + b3), (1, 2 * b2 + b3), (0, box(c[0], c[1], b2, b3), 2)) for b3 in range(2)]
            for b2 in range(2)
        ]
        return order.level([x, far], [early], jobs, after=after)

    def level7(c, keep, came, after):
        q = 2 * c[1] + c[0]
        jobs = [((r1, b3), (1 - r1, b3), (r1, (b3 * 4 + q, 0))) for b3 in range(2) for r1 in range(2)]
        return order.level([keep, came], [keep78, got1], [jobs], paired=True, after=after)[0]

    def level8(c, x, far):
        q = 2 * c[1] + c[0]
        jobs = [
            [((0, 2 * b3 + r1), (1, 2 * b3 + r1), (r1, (b3 * 4 + q, 1))) for r1 in range(2)]
            for b3 in range(2)
        ]
        return order.level([x, far], [keep78, got1], jobs)

    def late(c, r2, r1, l):
        q = 2 * c[1] + c[0]
        return ((0, (q, l)), (1, (8 + q, l)), (2, (q, l)), (3, (q, l)))[2 * r2 + r1]

    def level9(c, keep, came, after):
        jobs = [((r2, r1), (1 - r2, r1), late(c, r2, r1, 0)) for r1 in range(2) for r2 in range(2)]
        return order.level([keep, came], [keep9, got1, got2, got3], [jobs], paired=True, after=after)[0]

    def level10(c, x, far):
        jobs = [
            ((0, 2 * r1 + r2), (1, 2 * r1 + r2), late(c, r2, r1, 1)) for r2 in range(2) for r1 in range(2)
        ]
        return order.level([x, far], [keep9, got1, got2, got3], [jobs])[0]

    P0, Q0, P1, Q1 = (0, 1), (0, 0), (1, 1), (1, 0)
    near, far, keep, send, came, spread, fields = {}, {}, {}, {}, {}, {}, []

    facing = [swapped(h, "tgt", 1) for h in halves]

    def do4(b0):
        spread[b0] = level4(b0, facing[b0])
        far[b0] = swapped(spread[b0], "src", 1)

    def do5(b0, after):
        near[b0, 0], near[b0, 1] = level5(b0, spread[b0], far[b0], after)
        for b1 in (1, 0):
            far[b0, b1] = swapped(near[b0, b1], "tgt", 2)

    def do6(c, after=()):
        keep[c], send[c] = level6(c, near[c], far[c], after)
        came[c] = swapped(send[c], "src", 2)

    def do7(c, after=()):
        near[c] = level7(c, keep[c], came[c], after)
        far[c] = swapped(near[c], "tgt", 4)

    def do8(c):
        keep[c], send[c] = level8(c, near[c], far[c])
        came[c] = swapped(send[c], "src", 4)

    def do9(c, after=()):
        near[c] = level9(c, keep[c], came[c], after)
        far[c] = swapped(near[c], "tgt", 8)

    def do10(c):
        near[c] = level10(c, near[c], far[c])
        if c[1]:
            came[c] = swapped(near[c], "src", 1)

    def finish(b0):
        before = fields[-1] if fields else None
        fields.append(order.evaluated(evaluate, near[b0, 0], came[b0, 1], b0, before))

    two, quads = (0, 1), [(q & 1, q >> 1) for q in range(4)]
    plan = [((b0, b1, b2, 1), 9, b2, 2 * b1 + b0) for b0, b1 in quads for b2 in two]
    send2, send3 = order.split(weights, plan, (4, 4))
    do4(0), do4(1)
    plan = [((b0, b1, b2, b3), 7, b2, b3 * 4 + 2 * b1 + b0) for b2 in two for b3 in two for b0, b1 in quads]
    plan += [((b0, b1, 1, 0), 9, 1, 8 + 2 * b1 + b0) for b0, b1 in quads]
    plan += [((b0, b1, 0, 0), 9, 2, 2 * b1 + b0) for b0, b1 in quads]
    keep78, send1, keep9 = order.split(weights, plan, (8, 12, 4))
    got1, got2, got3 = swapped(send1, "src", 2), swapped(send2, "src", 4), swapped(send3, "src", 6)
    do5(0, ()), do5(1, ())
    do6(P0, (got1,)), do7(P0, (got2, got3)), do6(P1), do6(Q0), do7(P1), do8(P0), do7(Q0), do6(Q1)
    do9(P0), do8(P1), do7(Q1), do8(Q0), do9(P1), do9(Q0), do8(Q1), do10(P0)
    do10(P1), do9(Q1), do10(Q0), finish(0), do10(Q1), finish(1)
    field = fields[-1]
    return field[None]


def solution(mesh):
    placed = (
        P("src", "tgt", None, None, None),
        P("src", "tgt", None, None, None, None),
        P("tgt", "src", None, None, None),
    )
    return jax.shard_map(
        shards, mesh=mesh, in_specs=placed, out_specs=P("tgt", "src", None, None), check_vma=False
    )
```
